256 devices in a mesh: oi: 16 (over z, x_lo), oj: 8 (over y, core), vert: 2 (over x_hi).
Axes of the slice: x: 4 (x_hi: 2, x_lo: 2; x = x_hi * 2 + x_lo), y: 4, z: 8, core: 2. Of those that a mesh axis runs over, the one named last changes fastest.
Arguments:
- amplitudes: bfloat16 [16, 16, 1200, 1200], P('oi', 'oj'), may hold values from -0.23925781 to 0.23925781
- slabs: bfloat16 [4, 1200, 300], P(None, 'oi'), may hold values from -0.375 to 0.375
- occ_bins: int32 [16], replicated, may hold values from 0 to 63
- vir_bins: int32 [4], replicated, may hold values from 0 to 63
- occ_levels: float32 [64], replicated, may hold values from -2 to -0.3
- vir_levels: float32 [64], replicated, may hold values from 0.2 to 3
Outputs:
- amps_new: float32 [16, 16, 4, 4], P('oi', 'oj', 'vert')
- doubled: bfloat16 [16, 16, 4, 4], P('oi', 'oj', 'vert')
The draws below stay inside these ranges and needn't reach their ends.
All inputs are finite; a program needn't handle non-finite values.
Results may differ from the reference program's by a relative error of at most 0.01.
Values may be sent and summed in bfloat16 or wider, within the bound.
A program may use at most 128 MiB of HBM per device.

```python
import jax
import jax.numpy as jnp
from jax import lax

V = 1200
NQ = 300
WIN = 4
NBINS = 64
NO = 16


def set_ends(result, rng, smallest, high):
    dims = result.shape
    place = [jax.random.randint(jax.random.fold_in(rng, axis), (), 0, dims[axis]) for axis in range(len(dims))]
    result = result.at[tuple(place)].set(smallest)
    longest = dims.index(max(dims))
    place[longest] = (place[longest] + 1) % dims[longest]
    return result.at[tuple(place)].set(high)


def levels(own_key, dims, pieces, low, high):
    level, own = 1.0, jax.random.fold_in(own_key, 6)
    for dim, shards_of in pieces:
        steps = jnp.exp(jax.random.uniform(jax.random.fold_in(own, dim), (shards_of,), jnp.float32, low / len(pieces), high / len(pieces)))
        level = level * jnp.repeat(steps, dims[dim] // shards_of).reshape([-1 if axis == dim else 1 for axis in range(len(dims))])
    return level


def noise(stream_key, extent, width, most, split=(), dtype=jnp.bfloat16):
    array = width * jax.random.normal(stream_key, extent, jnp.float32)
    if split:
        array = array * levels(stream_key, extent, split, -0.22, 0.18)
    return jnp.clip(array, -most, most).astype(dtype)


def setup_inputs(seed: int = 0) -> dict:
    splits = jax.random.split(jax.random.key(seed), 7)
    return {
        "amplitudes": noise(splits[0], (NO, NO, V, V), 0.04, 0.23925781, ((0, 16), (1, 8))),
        "slabs": noise(splits[1], (WIN, V, NQ), NQ ** -0.5, 0.375, ((1, 16),)),
        "occ_bins": set_ends(jax.random.randint(splits[2], (NO,), 0, NBINS), jax.random.fold_in(splits[2], 1), 0, NBINS - 1).astype(jnp.int32),
        "vir_bins": set_ends(jax.random.randint(splits[3], (WIN,), 0, NBINS), jax.random.fold_in(splits[3], 1), 0, NBINS - 1).astype(jnp.int32),
        "occ_levels": jnp.clip(jax.random.uniform(splits[4], (NBINS,), jnp.float32, -2.0, -0.3), -2.0, -0.3),
        "vir_levels": jnp.clip(jax.random.uniform(splits[5], (NBINS,), jnp.float32, 0.2, 3.0), 0.2, 3.0),
    }


def reference(amplitudes, slabs, occ_bins, vir_bins, occ_levels, vir_levels):
    slab_float = slabs.astype(jnp.float32)
    flat_amps = amplitudes.reshape(NO * NO, V * V)

    def per_row(slab_row):
        integral = jnp.einsum('cq,bdq->bcd', slab_row, slab_float).astype(jnp.bfloat16)
        return jnp.dot(flat_amps, integral.reshape(WIN, V * V).T, preferred_element_type=jnp.float32)

    stacked = lax.map(per_row, slab_float)
    resid = jnp.transpose(stacked.reshape(WIN, NO, NO, WIN), (1, 2, 0, 3))
    sym = resid + jnp.transpose(resid, (1, 0, 3, 2))
    occ_energy = occ_levels[occ_bins]
    vir_energy = vir_levels[vir_bins]
    denom = occ_energy[:, None, None, None] + occ_energy[None, :, None, None] - vir_energy[None, None, :, None] - vir_energy[None, None, None, :]
    amps_new = sym / denom
    doubled = (2.0 * amps_new - jnp.transpose(amps_new, (1, 0, 2, 3))).astype(jnp.bfloat16)
    return (amps_new, doubled)
```

```python
import jax
import jax.numpy as jnp
from jax import lax
from jax.experimental import pallas as pl
from jax.experimental.pallas import tpu as pltpu
from jax.sharding import PartitionSpec as P

MESH = pl.DeviceIdType.MESH
LANES = 128
N_Z = 8
TAIL = 32
ORDER = (1, 7, 2, 6, 3, 5, 4)
GROUPS = ((0, 5), (5, 8))


def place_of(r):
    far = r // 5
    return (1 - far) * (2 * r - 1) + far * (16 - 2 * r) + (8 - r) // 8


def kernel(amps, slabs, occ_bins, vir_bins, occ_levels, vir_levels, out_new, out_two,
           t, own, ra, rb, rc, bf, bc, y, acc, mine, from_vert, from_pair,
           t_sem, own_sem, zs, zr, xs, xr, cs, cr, fs, fr):
    oi, oj, v = lax.axis_index("oi"), lax.axis_index("oj"), lax.axis_index("vert")
    z, xl, yy, c = oi // 2, oi % 2, oj // 2, oj % 2
    virt, full, aux = own.shape[0], amps.shape[2], own.shape[2]
    span = own.shape[1]
    bufs = (ra, rb, rc)

    own_copy = pltpu.make_async_copy(slabs, own, own_sem)
    own_copy.start()
    t_copies = []
    for p in range(2):
        cp = pltpu.make_async_copy(amps.at[0, p], t.at[p], t_sem.at[p])
        cp.start()
        t_copies.append(cp)

    def ring(d):
        return (lax.rem(z + d, N_Z) * 2 + xl, oj, v)

    across = (z * 2 + 1 - xl, oj, v)
    sibling = (oi, yy * 2 + 1 - c, v)
    peer = (oi, oj, 1 - v)
    diag = [(oj * 2 + p) == oi for p in range(2)]

    def pair(p, w):
        return (oj * 2 + p, oi // 2, w)

    barrier = pltpu.get_barrier_semaphore()
    for d in ORDER:
        pl.semaphore_signal(barrier, inc=1, device_id=ring(d), device_id_type=MESH)
    for who in (across, sibling, peer):
        pl.semaphore_signal(barrier, inc=1, device_id=who, device_id_type=MESH)
    for p in range(2):
        for dv in range(2):
            if dv == 1:
                pl.semaphore_signal(barrier, inc=1, device_id=pair(p, 1 - v), device_id_type=MESH)
            else:
                @pl.when(jnp.logical_not(diag[p]))
                def _(p=p):
                    pl.semaphore_signal(barrier, inc=1, device_id=pair(p, v), device_id_type=MESH)

    own_copy.wait()
    lane = lax.broadcasted_iota(jnp.int32, (80, LANES), 1)
    left = aux - 2 * LANES
    half_left = left // 2
    tail = jnp.zeros((80, LANES), jnp.float32)
    for a in range(virt):
        rows = own[a].astype(jnp.float32)
        rows = jnp.concatenate([rows, jnp.zeros((80 - span, aux), jnp.float32)], axis=0)
        main = jnp.where(v == 0, rows[:, :LANES], rows[:, LANES : 2 * LANES])
        bufs[a // 2][a % 2, xl, 0] = main.astype(jnp.bfloat16)
        rest = jnp.concatenate([rows[:, 2 * LANES :], jnp.zeros((80, LANES - left), jnp.float32)], axis=1)
        first = pltpu.roll(rest, TAIL * a, 1) if a else rest
        second = pltpu.roll(rest, (TAIL * a - half_left) % LANES, 1)
        moved = jnp.where(v == 0, first, second)
        tail = jnp.where((lane >= TAIL * a) & (lane < TAIL * a + half_left), moved, tail)
    rc[0, xl, 0] = tail[:48].astype(jnp.bfloat16)
    rc[1, xl, 0] = jnp.concatenate([tail[48:], jnp.zeros((16, LANES), jnp.float32)], axis=0).astype(jnp.bfloat16)

    is_diag = diag[0].astype(jnp.int32) + diag[1].astype(jnp.int32)
    pl.semaphore_wait(barrier, 14 - is_diag)

    def remote(src, dst, s, r, who):
        cp = pltpu.make_async_remote_copy(
            src_ref=src, dst_ref=dst, send_sem=s, recv_sem=r, device_id=who, device_id_type=MESH)
        cp.start()
        return cp

    sent = []
    z_copies = []
    for n, buf in enumerate(bufs):
        row = {}
        for d in ORDER:
            row[d] = remote(buf.at[c, xl, 0], buf.at[c, xl, place_of(N_Z - d)], zs.at[n, d - 1], zr.at[n, d - 1], ring(d))
            sent.append(row[d])
        z_copies.append(row)

    x_copies = [[None, None] for _ in bufs]
    c_copies = [[None] * 4 for _ in bufs]

    def after_z(n):
        buf = bufs[n]
        for g, (lo, hi) in enumerate(GROUPS):
            for d in ORDER:
                if lo <= place_of(N_Z - d) < hi:
                    z_copies[n][d].wait_recv()
            block = buf.at[c, xl, pl.ds(lo, hi - lo)]
            x_copies[n][g] = remote(block, block, xs.at[n, g], xr.at[n, g], across)
            lo = max(lo, 1)
            block = buf.at[c, xl, pl.ds(lo, hi - lo)]
            c_copies[n][g] = remote(block, block, cs.at[n, g], cr.at[n, g], sibling)
            sent.extend([x_copies[n][g], c_copies[n][g]])

    def after_x(n):
        buf = bufs[n]
        for g, (lo, hi) in enumerate(GROUPS):
            x_copies[n][g].wait_recv()
            block = buf.at[c, 1 - xl, pl.ds(lo, hi - lo)]
            c_copies[n][2 + g] = remote(block, block, cs.at[n, 2 + g], cr.at[n, 2 + g], sibling)
            sent.append(c_copies[n][2 + g])

    def after_c(n):
        for cp in c_copies[n]:
            cp.wait_recv()
        buf = bufs[n]
        for zz in range(N_Z):
            pos = place_of(lax.rem(zz - z + N_Z, N_Z))
            for half in range(2):
                at = (2 * zz + half) * span
                if n < 2:
                    for k in range(2):
                        bf[2 * n + k, at : at + span, :] = buf[k, half, pos][:span].astype(jnp.float32)
                else:
                    bf[4, at : at + 48, :] = buf[0, half, pos].astype(jnp.float32)
                    bf[4, at + 48 : at + span, :] = buf[1, half, pos][: span - 48].astype(jnp.float32)
        for a in range(2 * n, min(2 * n + 2, 5)):
            bc[:, LANES * a : LANES * (a + 1)] = bf[a].astype(jnp.bfloat16)

    def multiply(n):
        cols = slice(256 * n, min(256 * n + 256, 5 * LANES))
        for p in range(2):
            y[p, :, cols] = jnp.dot(t[p], bc[:, cols], preferred_element_type=jnp.float32)

    step = 80

    def fold(x):
        return jnp.sum(x.reshape(step // 8, 8, LANES), axis=0)

    after_z(0)
    after_z(1)
    after_x(0)
    after_z(2)
    after_x(1)
    acc[...] = jnp.zeros_like(acc)
    after_c(0)
    for cp in t_copies:
        cp.wait()
    multiply(0)
    after_x(2)
    after_c(1)
    multiply(1)

    @pl.loop(0, full // step)
    def _(s):
        rows = pl.ds(pl.multiple_of(s * step, 16), step)
        fac = [bf[a, rows, :] for a in range(4)]
        for p in range(2):
            for b in range(4):
                part = y[p, rows, LANES * b : LANES * (b + 1)]
                for a in range(4):
                    acc[p, a, b] += fold(part * fac[a])

    after_c(2)
    multiply(2)

    @pl.loop(0, full // step)
    def _(s):
        rows = pl.ds(pl.multiple_of(s * step, 16), step)
        fac = bf[4, rows, :]
        turned = [fac] + [pltpu.roll(fac, TAIL * d, 1) for d in range(1, 4)]
        for p in range(2):
            part = y[p, rows, 4 * LANES : 5 * LANES]
            for d in range(4):
                acc[p, 4, d] += fold(part * turned[d])

    lane = lax.broadcasted_iota(jnp.int32, (8, LANES), 1)
    for p in range(2):
        for a in range(4):
            for b in range(4):
                inside = (lane >= TAIL * b) & (lane < TAIL * (b + 1))
                total = acc[p, a, b] + jnp.where(inside, acc[p, 4, (b - a) % 4], 0.0)
                total = jnp.sum(total, axis=0, keepdims=True)
                mine[p, 4 * a + b : 4 * a + b + 1, :] = total
                mine[p, 16 + 4 * b + a : 16 + 4 * b + a + 1, :] = total
    for p in range(2):
        mine[p] = jnp.broadcast_to(jnp.sum(mine[p], axis=1, keepdims=True), (32, LANES))

    place = oi % 2
    to_vert = remote(mine, from_vert, fs.at[4], fr.at[2, 0], peer)
    sent.append(to_vert)
    for p in range(2):
        remote(mine.at[p], from_pair.at[place, v], fs.at[2 * p + 1], fr.at[place, v], pair(p, 1 - v))

        @pl.when(jnp.logical_not(diag[p]))
        def _(p=p):
            remote(mine.at[p], from_pair.at[place, v], fs.at[2 * p], fr.at[place, v], pair(p, v))

        @pl.when(diag[p])
        def _(p=p):
            pltpu.make_async_copy(mine.at[p], from_pair.at[p, v], fr.at[p, v]).start()

    row = lax.broadcasted_iota(jnp.int32, (16, LANES), 0)
    energy_i = occ_levels[occ_bins[oi]]
    ea = jnp.zeros((16, LANES), jnp.float32)
    eb = jnp.zeros((16, LANES), jnp.float32)
    for k in range(4):
        level = vir_levels[vir_bins[k]]
        ea = jnp.where(row // 4 == k, level, ea)
        eb = jnp.where(row % 4 == k, level, eb)

    to_vert.wait_recv()
    for p in range(2):
        for w in range(2):
            pltpu.make_async_copy(from_pair.at[p, w], from_pair.at[p, w], fr.at[p, w]).wait()
        here = mine[p] + from_vert[p]
        there = from_pair[p, 0] + from_pair[p, 1]
        denom = energy_i + occ_levels[occ_bins[oj * 2 + p]] - ea - eb
        new = (here[:16] + there[16:]) / denom
        swapped = (there[:16] + here[16:]) / denom
        two = 2.0 * new - swapped
        new = jnp.where(v == 0, new[:8], new[8:])
        two = jnp.where(v == 0, two[:8], two[8:])
        keep = lane == lax.broadcasted_iota(jnp.int32, (8, LANES), 0) % 4

        def spread(x):
            x = jnp.where(keep, x, 0.0)
            return jnp.concatenate(
                [jnp.sum(x[:4], axis=0, keepdims=True), jnp.sum(x[4:], axis=0, keepdims=True)], axis=0)[:, :4]

        out_new[0, p] = spread(new)
        out_two[0, p] = spread(two).astype(jnp.bfloat16)

    for cp in sent:
        cp.wait_send()
    for p in range(2):
        pltpu.make_async_copy(mine.at[p], mine.at[p], fs.at[2 * p + 1]).wait()

        @pl.when(jnp.logical_not(diag[p]))
        def _(p=p):
            pltpu.make_async_copy(mine.at[p], mine.at[p], fs.at[2 * p]).wait()


def on_device(amplitudes, slabs, occ_bins, vir_bins, occ_levels, vir_levels):
    full = amplitudes.shape[2]
    bf16, f32 = jnp.bfloat16, jnp.float32
    dma, vmem = pltpu.SemaphoreType.DMA, pltpu.VMEM
    any_space = pl.BlockSpec(memory_space=pl.ANY)
    smem = pl.BlockSpec(memory_space=pltpu.SMEM)
    return pl.pallas_call(
        kernel,
        out_shape=(jax.ShapeDtypeStruct((1, 2, 2, 4), f32), jax.ShapeDtypeStruct((1, 2, 2, 4), bf16)),
        in_specs=[any_space, any_space, smem, smem, smem, smem],
        out_specs=(pl.BlockSpec(memory_space=pltpu.VMEM), pl.BlockSpec(memory_space=pltpu.VMEM)),
        scratch_shapes=[
            vmem((2, full, full), bf16),
            vmem(slabs.shape, bf16),
            vmem((2, 2, N_Z, 80, LANES), bf16),
            vmem((2, 2, N_Z, 80, LANES), bf16),
            vmem((2, 2, N_Z, 48, LANES), bf16),
            vmem((5, full, LANES), f32),
            vmem((full, 5 * LANES), bf16),
            vmem((2, full, 5 * LANES), f32),
            vmem((2, 5, 4, 8, LANES), f32),
            vmem((2, 32, LANES), f32),
            vmem((2, 32, LANES), f32),
            vmem((2, 2, 32, LANES), f32),
            dma((2,)), dma,
            dma((3, 7)), dma((3, 7)),
            dma((3, 2)), dma((3, 2)),
            dma((3, 4)), dma((3, 4)),
            dma((5,)), dma((3, 2)),
        ],
        compiler_params=pltpu.CompilerParams(
            collective_id=0, has_side_effects=True, vmem_limit_bytes=48 << 20),
    )(amplitudes, slabs, occ_bins, vir_bins, occ_levels, vir_levels)


def solution(mesh):
    return jax.shard_map(
        on_device,
        mesh=mesh,
        in_specs=(P("oi", "oj", None, None), P(None, "oi", None), P(), P(), P(), P()),
        out_specs=(P("oi", "oj", "vert", None), P("oi", "oj", "vert", None)),
        check_vma=False,
    )
```

```python
import jax
import jax.numpy as jnp
from jax import lax
from jax.experimental import pallas as pl
from jax.experimental.pallas import tpu as pltpu
from jax.sharding import PartitionSpec as P

MESH = pl.DeviceIdType.MESH
LANES = 128
N_Z = 8
TAIL = 32
EARLY = (False, False, True)
GROUPS = ((0, 1), (1, 5), (5, 8))
STEPS = (1, -1, 2, -2)


def place_of(r):
    far = r // 5
    return (1 - far) * (2 * r - 1) + far * (16 - 2 * r) + (8 - r) // 8


def kernel(amps, slabs, occ_bins_in, vir_bins_in, occ_levels_in, vir_levels_in, out,
           occ_bins, vir_bins, occ_levels, vir_levels, small_sem, t, own, ra, rb, rc, bf, bc, y, acc, mine, from_vert, from_pair,
           t_sem, own_sem, zs, zr, xs, xr, cs, cr, fs, fr):
    oi, oj, v = lax.axis_index("oi"), lax.axis_index("oj"), lax.axis_index("vert")
    z, xl, yy, c = oi // 2, oi % 2, oj // 2, oj % 2
    span, virt, aux = own.shape
    full = amps.shape[2]
    bufs = (ra, rb, rc)

    def ring(d, line):
        return (lax.rem(z + d + N_Z, N_Z) * 2 + line, oj, v)

    across = (z * 2 + 1 - xl, oj, v)
    sibling = (oi, yy * 2 + 1 - c, v)
    peer = (oi, oj, 1 - v)
    diag = [(oj * 2 + p) == oi for p in range(2)]

    def pair(p, w):
        return (oj * 2 + p, oi // 2, w)

    barrier = pltpu.get_barrier_semaphore()
    near = [ring(d, xl) for d in STEPS] + [across, sibling, peer]
    if any(EARLY):
        near += [ring(d, 1 - xl) for d in STEPS]
    for who in near:
        pl.semaphore_signal(barrier, inc=1, device_id=who, device_id_type=MESH)

    hub = oj == z
    for line in range(2):
        for w in range(2):
            @pl.when(jnp.logical_not(hub & (line == xl) & (w == v)))
            def _(line=line, w=w):
                pl.semaphore_signal(barrier, inc=1, device_id=(z * 2 + line, z, w), device_id_type=MESH)

    own_copy = pltpu.make_async_copy(slabs, own, own_sem)
    own_copy.start()
    small = []
    for k, (src, dst) in enumerate((
            (occ_bins_in, occ_bins), (vir_bins_in, vir_bins), (occ_levels_in, occ_levels), (vir_levels_in, vir_levels))):
        cp = pltpu.make_async_copy(src, dst, small_sem.at[k])
        cp.start()
        small.append(cp)
    t_copies = []
    for p in range(2):
        cp = pltpu.make_async_copy(amps.at[0, p], t.at[p], t_sem.at[p])
        cp.start()
        t_copies.append(cp)

    own_copy.wait()
    wide_own = own[...].astype(jnp.float32)
    lane = lax.broadcasted_iota(jnp.int32, (80, LANES), 1)
    left = aux - 2 * LANES
    half_left = left // 2
    tail = jnp.zeros((80, LANES), jnp.float32)
    for a in range(virt):
        rows = wide_own[:, a, :]
        rows = jnp.concatenate([rows, jnp.zeros((80 - span, aux), jnp.float32)], axis=0)
        main = jnp.where(v == 0, rows[:, :LANES], rows[:, LANES : 2 * LANES])
        bufs[a // 2][a % 2, xl, 0] = main.astype(jnp.bfloat16)
        rest = jnp.concatenate([rows[:, 2 * LANES :], jnp.zeros((80, LANES - left), jnp.float32)], axis=1)
        first = pltpu.roll(rest, TAIL * a, 1) if a else rest
        second = pltpu.roll(rest, (TAIL * a - half_left) % LANES, 1)
        moved = jnp.where(v == 0, first, second)
        tail = jnp.where((lane >= TAIL * a) & (lane < TAIL * a + half_left), moved, tail)
    rc[0, xl, 0] = tail[:48].astype(jnp.bfloat16)
    rc[1, xl, 0] = jnp.concatenate([tail[48:], jnp.zeros((16, LANES), jnp.float32)], axis=0).astype(jnp.bfloat16)

    pl.semaphore_wait(barrier, len(near) + 31 * hub.astype(jnp.int32))

    def remote(src, dst, s, r, who):
        cp = pltpu.make_async_remote_copy(
            src_ref=src, dst_ref=dst, send_sem=s, recv_sem=r, device_id=who, device_id_type=MESH)
        cp.start()
        return cp

    sent = []

    def send(src, dst, s, r, who):
        sent.append(remote(src, dst, s, r, who))
        return sent[-1]

    x_copies = [[None] * 3 for _ in bufs]
    c_copies = [[] for _ in bufs]
    z_first, z_second = [], []

    def to_sibling(n, block):
        k = len(c_copies[n])
        c_copies[n].append(send(block, block, cs.at[n, k], cr.at[n, k], sibling))

    def x_send(n, g):
        lo, hi = GROUPS[g]
        block = bufs[n].at[c, xl, pl.ds(lo, hi - lo)]
        x_copies[n][g] = send(block, block, xs.at[n, g], xr.at[n, g], across)

    def start(n):
        buf, row = bufs[n], []
        for k, d in enumerate(STEPS):
            row.append(send(buf.at[c, xl, 0], buf.at[c, xl, place_of(-d % N_Z)], zs.at[n, k], zr.at[n, k], ring(d, xl)))
        x_send(n, 0)
        if EARLY[n]:
            for k, d in enumerate(STEPS):
                row.append(send(
                    buf.at[c, xl, 0], buf.at[c, xl, place_of(-d % N_Z)], zs.at[n, 7 + k], zr.at[n, 7 + k], ring(d, 1 - xl)))
        z_first.append(row)

    def after_first(n):
        buf = bufs[n]
        for cp in z_first[n]:
            cp.wait_recv()
        lines = pl.ds(0, 2) if EARLY[n] else pl.ds(xl, 1)
        back, ahead = place_of(6), place_of(2)
        row = [
            send(buf.at[c, lines, back], buf.at[c, lines, place_of(5)], zs.at[n, 4], zr.at[n, 4], ring(1, xl)),
            send(buf.at[c, lines, ahead], buf.at[c, lines, place_of(3)], zs.at[n, 5], zr.at[n, 5], ring(-1, xl)),
            send(buf.at[c, lines, back + c * (ahead - back)], buf.at[c, lines, place_of(4)],
                 zs.at[n, 6], zr.at[n, 6], ring(2 - 4 * c, xl)),
        ]
        z_second.append(row)
        if not EARLY[n]:
            x_send(n, 1)
        to_sibling(n, buf.at[c, lines, pl.ds(1, 4)])

    def after_second(n):
        buf = bufs[n]
        for cp in z_second[n]:
            cp.wait_recv()
        lines = pl.ds(0, 2) if EARLY[n] else pl.ds(xl, 1)
        if not EARLY[n]:
            x_send(n, 2)
        to_sibling(n, buf.at[c, lines, pl.ds(5, 3)])

    def after_x(n, g):
        x_copies[n][g].wait_recv()
        lo, hi = GROUPS[g]
        to_sibling(n, bufs[n].at[c, 1 - xl, pl.ds(lo, hi - lo)])

    def after_c(n):
        for cp in c_copies[n]:
            cp.wait_recv()
        buf = bufs[n]
        for zz in range(N_Z):
            pos = place_of(lax.rem(zz - z + N_Z, N_Z))
            for half in range(2):
                at = (2 * zz + half) * span
                if n < 2:
                    for k in range(2):
                        bf[2 * n + k, at : at + span, :] = buf[k, half, pos][:span].astype(jnp.float32)
                else:
                    bf[4, at : at + 48, :] = buf[0, half, pos].astype(jnp.float32)
                    bf[4, at + 48 : at + span, :] = buf[1, half, pos][: span - 48].astype(jnp.float32)
        for a in range(2 * n, min(2 * n + 2, 5)):
            bc[:, LANES * a : LANES * (a + 1)] = bf[a].astype(jnp.bfloat16)

    def fold(x):
        return jnp.sum(x.reshape(full // 8, 8, LANES), axis=0)

    def product(p, n):
        cols = slice(256 * n, min(256 * n + 256, 5 * LANES))
        return jnp.dot(t[p], bc[:, cols], preferred_element_type=jnp.float32)

    def contract_main():
        for p in range(2):
            late = product(p, 1)
            for b in range(4):
                part = y[p, :, LANES * b : LANES * (b + 1)] if b < 2 else late[:, LANES * (b - 2) : LANES * (b - 1)]
                for a in range(4):
                    acc[p, a, b] = fold(part * bf[a])

    def contract_tail():
        for p in range(2):
            part = product(p, 2)
            for d in range(4):
                acc[p, 4, d] = fold(part * (pltpu.roll(bf[4], TAIL * d, 1) if d else bf[4]))

    for n in range(3):
        start(n)
    after_x(0, 0)
    after_first(0)
    after_x(1, 0)
    after_first(1)
    after_x(2, 0)
    after_first(2)
    after_second(0)
    after_x(0, 1)
    after_second(1)
    after_x(0, 2)
    after_second(2)
    after_x(1, 1)
    for cp in t_copies:
        cp.wait()
    after_c(0)
    after_x(1, 2)
    for p in range(2):
        y[p] = product(p, 0)
    after_c(1)
    contract_main()
    after_c(2)
    contract_tail()

    lane = lax.broadcasted_iota(jnp.int32, (8, LANES), 1)
    wide = lax.broadcasted_iota(jnp.int32, (16, LANES), 1)
    row = lax.broadcasted_iota(jnp.int32, (16, LANES), 0)
    keep = (wide == row) | (wide == 16 + 4 * (row % 4) + row // 4)
    for p in range(2):
        rows = []
        for a in range(4):
            for b in range(4):
                inside = (lane >= TAIL * b) & (lane < TAIL * (b + 1))
                total = acc[p, a, b] + jnp.where(inside, acc[p, 4, (b - a) % 4], 0.0)
                rows.append(jnp.sum(total, axis=0, keepdims=True))
        total = jnp.sum(jnp.concatenate(rows, axis=0), axis=1, keepdims=True)
        mine[p] = jnp.broadcast_to(jnp.sum(jnp.where(keep, total, 0.0), axis=0, keepdims=True), (8, LANES))

    place = oi % 2
    to_vert = remote(mine, from_vert, fs.at[4], fr.at[2, 0], peer)
    sent.append(to_vert)
    for p in range(2):
        remote(mine.at[p], from_pair.at[place, v], fs.at[2 * p + 1], fr.at[place, v], pair(p, 1 - v))

        @pl.when(jnp.logical_not(diag[p]))
        def _(p=p):
            remote(mine.at[p], from_pair.at[place, v], fs.at[2 * p], fr.at[place, v], pair(p, v))

        @pl.when(diag[p])
        def _(p=p):
            pltpu.make_async_copy(mine.at[p], from_pair.at[p, v], fr.at[p, v]).start()

    for cp in small:
        cp.wait()
    energy_i = occ_levels[occ_bins[oi]]
    ea = jnp.zeros((8, LANES), jnp.float32)
    eb = jnp.zeros((8, LANES), jnp.float32)
    for k in range(4):
        level = vir_levels[vir_bins[k]]
        ea = jnp.where(lane // 4 == k, level, ea)
        eb = jnp.where(lane % 4 == k, level, eb)

    to_vert.wait_recv()
    for p in range(2):
        for w in range(2):
            pltpu.make_async_copy(from_pair.at[p, w], from_pair.at[p, w], fr.at[p, w]).wait()
        here = mine[p] + from_vert[p]
        there = from_pair[p, 0] + from_pair[p, 1]
        denom = energy_i + occ_levels[occ_bins[oj * 2 + p]] - ea - eb
        new = (here + pltpu.roll(there, LANES - 16, 1)) / denom
        swapped = (there + pltpu.roll(here, LANES - 16, 1)) / denom
        two = 2.0 * new - swapped

        def spread(x):
            x = jnp.where(v == 0, x, pltpu.roll(x, LANES - 8, 1))
            x = jnp.where(lax.broadcasted_iota(jnp.int32, (8, LANES), 0) == 0, x, pltpu.roll(x, LANES - 4, 1))
            return x[:2, :4]

        out[0, 0, p] = spread(new)
        out[1, 0, p] = spread(swapped)

    for cp in sent:
        cp.wait_send()
    for p in range(2):
        pltpu.make_async_copy(mine.at[p], mine.at[p], fs.at[2 * p + 1]).wait()

        @pl.when(jnp.logical_not(diag[p]))
        def _(p=p):
            pltpu.make_async_copy(mine.at[p], mine.at[p], fs.at[2 * p]).wait()


def on_device(amplitudes, slabs, occ_bins, vir_bins, occ_levels, vir_levels):
    full = amplitudes.shape[2]
    bf16, f32 = jnp.bfloat16, jnp.float32
    dma, vmem = pltpu.SemaphoreType.DMA, pltpu.VMEM
    any_space = pl.BlockSpec(memory_space=pltpu.HBM)
    smem = pltpu.SMEM
    both = pl.pallas_call(
        kernel,
        out_shape=jax.ShapeDtypeStruct((2, 1, 2, 2, 4), f32),
        in_specs=[any_space] * 6,
        out_specs=pl.BlockSpec(memory_space=pltpu.VMEM),
        scratch_shapes=[
            smem(occ_bins.shape, jnp.int32), smem(vir_bins.shape, jnp.int32),
            smem(occ_levels.shape, f32), smem(vir_levels.shape, f32),
            dma((4,)),
            vmem((2, full, full), bf16),
            vmem((slabs.shape[1], slabs.shape[0], slabs.shape[2]), bf16),
            vmem((2, 2, N_Z, 80, LANES), bf16),
            vmem((2, 2, N_Z, 80, LANES), bf16),
            vmem((2, 2, N_Z, 48, LANES), bf16),
            vmem((5, full, LANES), f32),
            vmem((full, 5 * LANES), bf16),
            vmem((2, full, 2 * LANES), f32),
            vmem((2, 5, 4, 8, LANES), f32),
            vmem((2, 8, LANES), f32),
            vmem((2, 8, LANES), f32),
            vmem((2, 2, 8, LANES), f32),
            dma((2,)), dma,
            dma((3, 11)), dma((3, 11)),
            dma((3, 3)), dma((3, 3)),
            dma((3, 5)), dma((3, 5)),
            dma((5,)), dma((3, 2)),
        ],
        compiler_params=pltpu.CompilerParams(
            collective_id=0, has_side_effects=True, vmem_limit_bytes=56 << 20),
    )(amplitudes, jnp.transpose(slabs, (1, 0, 2)), occ_bins, vir_bins, occ_levels, vir_levels)
    return both[0], (2.0 * both[0] - both[1]).astype(bf16)


def solution(mesh):
    return jax.shard_map(
        on_device,
        mesh=mesh,
        in_specs=(P("oi", "oj", None, None), P(None, "oi", None), P(), P(), P(), P()),
        out_specs=(P("oi", "oj", "vert", None), P("oi", "oj", "vert", None)),
        check_vma=False,
    )
```

```python
import jax
import jax.numpy as jnp
from jax import lax
from jax.experimental import pallas as pl
from jax.experimental.pallas import tpu as pltpu
from jax.sharding import PartitionSpec as P

MESH = pl.DeviceIdType.MESH
LANES = 128
N_Z = 8
TAIL = 32
EARLY = (False, False, False)
GROUPS = ((0, 1), (1, 5), (5, 8))
STEPS = (1, -1, 2, -2)


def place_of(r):
    far = r // 5
    return (1 - far) * (2 * r - 1) + far * (16 - 2 * r) + (8 - r) // 8


def kernel(amps, slabs, occ_bins_in, vir_bins_in, occ_levels_in, vir_levels_in, out,
           occ_bins, vir_bins, occ_levels, vir_levels, small_sem, t, own, ra, rb, rc, bf, bc, y, acc, mine, from_vert, from_pair,
           t_sem, own_sem, zs, zr, xs, xr, cs, cr, fs, fr):
    oi, oj, v = lax.axis_index("oi"), lax.axis_index("oj"), lax.axis_index("vert")
    z, xl, yy, c = oi // 2, oi % 2, oj // 2, oj % 2
    span, virt, aux = own.shape
    full = amps.shape[2]
    bufs = (ra, rb, rc)

    def ring(d, line):
        return (lax.rem(z + d + N_Z, N_Z) * 2 + line, oj, v)

    across = (z * 2 + 1 - xl, oj, v)
    sibling = (oi, yy * 2 + 1 - c, v)
    peer = (oi, oj, 1 - v)
    diag = [(oj * 2 + p) == oi for p in range(2)]

    def pair(p, w):
        return (oj * 2 + p, oi // 2, w)

    barrier = pltpu.get_barrier_semaphore()
    near = [ring(d, xl) for d in STEPS] + [across, sibling, peer]
    if any(EARLY):
        near += [ring(d, 1 - xl) for d in STEPS]
    for who in near:
        pl.semaphore_signal(barrier, inc=1, device_id=who, device_id_type=MESH)

    hub = oj == z
    for line in range(2):
        for w in range(2):
            @pl.when(jnp.logical_not(hub & (line == xl) & (w == v)))
            def _(line=line, w=w):
                pl.semaphore_signal(barrier, inc=1, device_id=(z * 2 + line, z, w), device_id_type=MESH)

    own_copy = pltpu.make_async_copy(slabs, own, own_sem)
    own_copy.start()
    small = []
    for k, (src, dst) in enumerate((
            (occ_bins_in, occ_bins), (vir_bins_in, vir_bins), (occ_levels_in, occ_levels), (vir_levels_in, vir_levels))):
        cp = pltpu.make_async_copy(src, dst, small_sem.at[k])
        cp.start()
        small.append(cp)
    own_copy.wait()
    wide_own = own[...].astype(jnp.float32)
    lane = lax.broadcasted_iota(jnp.int32, (80, LANES), 1)
    left = aux - 2 * LANES
    half_left = left // 2
    tail = jnp.zeros((80, LANES), jnp.float32)
    for a in range(virt):
        rows = wide_own[:, a, :]
        rows = jnp.concatenate([rows, jnp.zeros((80 - span, aux), jnp.float32)], axis=0)
        main = jnp.where(v == 0, rows[:, :LANES], rows[:, LANES : 2 * LANES])
        bufs[a // 2][a % 2, xl, 0] = main.astype(jnp.bfloat16)
        rest = jnp.concatenate([rows[:, 2 * LANES :], jnp.zeros((80, LANES - left), jnp.float32)], axis=1)
        first = pltpu.roll(rest, TAIL * a, 1) if a else rest
        second = pltpu.roll(rest, (TAIL * a - half_left) % LANES, 1)
        moved = jnp.where(v == 0, first, second)
        tail = jnp.where((lane >= TAIL * a) & (lane < TAIL * a + half_left), moved, tail)
    rc[0, xl, 0] = tail[:48].astype(jnp.bfloat16)
    rc[1, xl, 0] = jnp.concatenate([tail[48:], jnp.zeros((16, LANES), jnp.float32)], axis=0).astype(jnp.bfloat16)

    pl.semaphore_wait(barrier, len(near) + 31 * hub.astype(jnp.int32))

    def remote(src, dst, s, r, who):
        cp = pltpu.make_async_remote_copy(
            src_ref=src, dst_ref=dst, send_sem=s, recv_sem=r, device_id=who, device_id_type=MESH)
        cp.start()
        return cp

    sent = []

    def send(src, dst, s, r, who):
        sent.append(remote(src, dst, s, r, who))
        return sent[-1]

    x_copies = [[None] * 3 for _ in bufs]
    c_copies = [[] for _ in bufs]
    z_first, z_second = {}, {}

    def to_sibling(n, block):
        k = len(c_copies[n])
        c_copies[n].append(send(block, block, cs.at[n, k], cr.at[n, k], sibling))

    def x_send(n, g):
        lo, hi = GROUPS[g]
        block = bufs[n].at[c, xl, pl.ds(lo, hi - lo)]
        x_copies[n][g] = send(block, block, xs.at[n, g], xr.at[n, g], across)

    def start(n):
        buf, row = bufs[n], []
        for k, d in enumerate(STEPS):
            row.append(send(buf.at[c, xl, 0], buf.at[c, xl, place_of(-d % N_Z)], zs.at[n, k], zr.at[n, k], ring(d, xl)))
        x_send(n, 0)
        if EARLY[n]:
            for k, d in enumerate(STEPS):
                row.append(send(
                    buf.at[c, xl, 0], buf.at[c, xl, place_of(-d % N_Z)], zs.at[n, 7 + k], zr.at[n, 7 + k], ring(d, 1 - xl)))
        z_first[n] = row

    def after_first(n):
        buf = bufs[n]
        for cp in z_first[n]:
            cp.wait_recv()
        lines = pl.ds(0, 2) if EARLY[n] else pl.ds(xl, 1)
        back, ahead = place_of(6), place_of(2)
        row = [
            send(buf.at[c, lines, back], buf.at[c, lines, place_of(5)], zs.at[n, 4], zr.at[n, 4], ring(1, xl)),
            send(buf.at[c, lines, ahead], buf.at[c, lines, place_of(3)], zs.at[n, 5], zr.at[n, 5], ring(-1, xl)),
            send(buf.at[c, lines, back + c * (ahead - back)], buf.at[c, lines, place_of(4)],
                 zs.at[n, 6], zr.at[n, 6], ring(2 - 4 * c, xl)),
        ]
        z_second[n] = row
        if not EARLY[n]:
            x_send(n, 1)
        to_sibling(n, buf.at[c, lines, pl.ds(1, 4)])

    def after_second(n):
        buf = bufs[n]
        for cp in z_second[n]:
            cp.wait_recv()
        lines = pl.ds(0, 2) if EARLY[n] else pl.ds(xl, 1)
        if not EARLY[n]:
            x_send(n, 2)
        to_sibling(n, buf.at[c, lines, pl.ds(5, 3)])

    def after_x(n, g):
        x_copies[n][g].wait_recv()
        lo, hi = GROUPS[g]
        to_sibling(n, bufs[n].at[c, 1 - xl, pl.ds(lo, hi - lo)])

    def after_c(n):
        for cp in c_copies[n]:
            cp.wait_recv()
        buf = bufs[n]
        for zz in range(N_Z):
            pos = place_of(lax.rem(zz - z + N_Z, N_Z))
            for half in range(2):
                at = (2 * zz + half) * span
                if n < 2:
                    for k in range(2):
                        bf[2 * n + k, at : at + span, :] = buf[k, half, pos][:span].astype(jnp.float32)
                else:
                    bf[4, at : at + 48, :] = buf[0, half, pos].astype(jnp.float32)
                    bf[4, at + 48 : at + span, :] = buf[1, half, pos][: span - 48].astype(jnp.float32)
        for a in range(2 * n, min(2 * n + 2, 5)):
            bc[:, LANES * a : LANES * (a + 1)] = bf[a].astype(jnp.bfloat16)

    def fold(x):
        return jnp.sum(x.reshape(full // 8, 8, LANES), axis=0)

    def product(p, n):
        cols = slice(256 * n, min(256 * n + 256, 5 * LANES))
        return jnp.dot(t[p], bc[:, cols], preferred_element_type=jnp.float32)

    def contract_main():
        for p in range(2):
            late = product(p, 1)
            for b in range(4):
                part = y[p, :, LANES * b : LANES * (b + 1)] if b < 2 else late[:, LANES * (b - 2) : LANES * (b - 1)]
                for a in range(4):
                    acc[p, a, b] = fold(part * bf[a])

    def contract_tail():
        for p in range(2):
            part = product(p, 2)
            for d in range(4):
                acc[p, 4, d] = fold(part * (pltpu.roll(bf[4], TAIL * d, 1) if d else bf[4]))

    for n in (0, 1, 2):
        start(n)
    t_copies = []
    for p in range(2):
        cp = pltpu.make_async_copy(amps.at[0, p], t.at[p], t_sem.at[p])
        cp.start()
        t_copies.append(cp)
    after_x(0, 0)
    after_first(0)
    after_x(1, 0)
    after_first(1)
    after_x(2, 0)
    after_first(2)
    after_second(0)
    after_x(0, 1)
    after_second(1)
    after_x(1, 1)
    after_second(2)
    after_x(2, 1)
    after_x(0, 2)
    after_x(1, 2)
    after_x(2, 2)
    for cp in t_copies:
        cp.wait()
    after_c(0)
    after_c(1)
    after_c(2)
    for p in range(2):
        y[p] = product(p, 0)
    contract_main()
    contract_tail()

    lane = lax.broadcasted_iota(jnp.int32, (8, LANES), 1)
    wide = lax.broadcasted_iota(jnp.int32, (16, LANES), 1)
    row = lax.broadcasted_iota(jnp.int32, (16, LANES), 0)
    keep = (wide == row) | (wide == 16 + 4 * (row % 4) + row // 4)
    for p in range(2):
        rows = []
        for a in range(4):
            for b in range(4):
                inside = (lane >= TAIL * b) & (lane < TAIL * (b + 1))
                total = acc[p, a, b] + jnp.where(inside, acc[p, 4, (b - a) % 4], 0.0)
                rows.append(jnp.sum(total, axis=0, keepdims=True))
        total = jnp.sum(jnp.concatenate(rows, axis=0), axis=1, keepdims=True)
        mine[p] = jnp.broadcast_to(jnp.sum(jnp.where(keep, total, 0.0), axis=0, keepdims=True), (8, LANES))

    place = oi % 2
    to_vert = remote(mine, from_vert, fs.at[4], fr.at[2, 0], peer)
    sent.append(to_vert)
    for p in range(2):
        remote(mine.at[p], from_pair.at[place, v], fs.at[2 * p + 1], fr.at[place, v], pair(p, 1 - v))

        @pl.when(jnp.logical_not(diag[p]))
        def _(p=p):
            remote(mine.at[p], from_pair.at[place, v], fs.at[2 * p], fr.at[place, v], pair(p, v))

        @pl.when(diag[p])
        def _(p=p):
            pltpu.make_async_copy(mine.at[p], from_pair.at[p, v], fr.at[p, v]).start()

    for cp in small:
        cp.wait()
    energy_i = occ_levels[occ_bins[oi]]
    ea = jnp.zeros((8, LANES), jnp.float32)
    eb = jnp.zeros((8, LANES), jnp.float32)
    for k in range(4):
        level = vir_levels[vir_bins[k]]
        ea = jnp.where(lane // 4 == k, level, ea)
        eb = jnp.where(lane % 4 == k, level, eb)

    to_vert.wait_recv()
    for p in range(2):
        for w in range(2):
            pltpu.make_async_copy(from_pair.at[p, w], from_pair.at[p, w], fr.at[p, w]).wait()
        here = mine[p] + from_vert[p]
        there = from_pair[p, 0] + from_pair[p, 1]
        denom = energy_i + occ_levels[occ_bins[oj * 2 + p]] - ea - eb
        new = (here + pltpu.roll(there, LANES - 16, 1)) / denom
        swapped = (there + pltpu.roll(here, LANES - 16, 1)) / denom
        two = 2.0 * new - swapped

        def spread(x):
            x = jnp.where(v == 0, x, pltpu.roll(x, LANES - 8, 1))
            x = jnp.where(lax.broadcasted_iota(jnp.int32, (8, LANES), 0) == 0, x, pltpu.roll(x, LANES - 4, 1))
            return x[:2, :4]

        out[0, 0, p] = spread(new)
        out[1, 0, p] = spread(swapped)

    for cp in sent:
        cp.wait_send()
    for p in range(2):
        pltpu.make_async_copy(mine.at[p], mine.at[p], fs.at[2 * p + 1]).wait()

        @pl.when(jnp.logical_not(diag[p]))
        def _(p=p):
            pltpu.make_async_copy(mine.at[p], mine.at[p], fs.at[2 * p]).wait()


def on_device(amplitudes, slabs, occ_bins, vir_bins, occ_levels, vir_levels):
    full = amplitudes.shape[2]
    bf16, f32 = jnp.bfloat16, jnp.float32
    dma, vmem = pltpu.SemaphoreType.DMA, pltpu.VMEM
    any_space = pl.BlockSpec(memory_space=pltpu.HBM)
    smem = pltpu.SMEM
    both = pl.pallas_call(
        kernel,
        out_shape=pltpu.VMEM((2, 1, 2, 2, 4), f32),
        in_specs=[any_space] * 6,
        out_specs=pl.BlockSpec(memory_space=pltpu.VMEM),
        scratch_shapes=[
            smem(occ_bins.shape, jnp.int32), smem(vir_bins.shape, jnp.int32),
            smem(occ_levels.shape, f32), smem(vir_levels.shape, f32),
            dma((4,)),
            vmem((2, full, full), bf16),
            vmem((slabs.shape[1], slabs.shape[0], slabs.shape[2]), bf16),
            vmem((2, 2, N_Z, 80, LANES), bf16),
            vmem((2, 2, N_Z, 80, LANES), bf16),
            vmem((2, 2, N_Z, 48, LANES), bf16),
            vmem((5, full, LANES), f32),
            vmem((full, 5 * LANES), bf16),
            vmem((2, full, 2 * LANES), f32),
            vmem((2, 5, 4, 8, LANES), f32),
            vmem((2, 8, LANES), f32),
            vmem((2, 8, LANES), f32),
            vmem((2, 2, 8, LANES), f32),
            dma((2,)), dma,
            dma((3, 11)), dma((3, 11)),
            dma((3, 3)), dma((3, 3)),
            dma((3, 5)), dma((3, 5)),
            dma((5,)), dma((3, 2)),
        ],
        compiler_params=pltpu.CompilerParams(
            collective_id=0, has_side_effects=True, vmem_limit_bytes=56 << 20),
    )(amplitudes, jnp.transpose(slabs, (1, 0, 2)), occ_bins, vir_bins, occ_levels, vir_levels)
    return both[0], (2.0 * both[0] - both[1]).astype(bf16)


def solution(mesh):
    return jax.shard_map(
        on_device,
        mesh=mesh,
        in_specs=(P("oi", "oj", None, None), P(None, "oi", None), P(), P(), P(), P()),
        out_specs=(P("oi", "oj", "vert", None), P("oi", "oj", "vert", None)),
        check_vma=False,
    )
```

```python
import jax
import jax.numpy as jnp
from jax import lax
from jax.experimental import pallas as pl
from jax.experimental.pallas import tpu as pltpu
from jax.sharding import PartitionSpec as P

MESH = pl.DeviceIdType.MESH
LANES = 128
N_Z = 8
TAIL = 32
EARLY = (False, False, False)
GROUPS = ((0, 1), (1, 5), (5, 8))
STEPS = (2, -2, 1, -1)


def place_of(r):
    far = r // 5
    return (1 - far) * (2 * r - 1) + far * (16 - 2 * r) + (8 - r) // 8


def kernel(amps, slabs, occ_bins_in, vir_bins_in, occ_levels_in, vir_levels_in, out,
           occ_bins, vir_bins, occ_levels, vir_levels, small_sem, t, own, ra, rb, rc, bf, bc, acc, mine, from_vert, from_pair,
           t_sem, own_sem, zs, zr, xs, xr, cs, cr, fs, fr):
    oi, oj, v = lax.axis_index("oi"), lax.axis_index("oj"), lax.axis_index("vert")
    z, xl, yy, c = oi // 2, oi % 2, oj // 2, oj % 2
    span, virt, aux = own.shape
    full = amps.shape[2]
    bufs = (ra, rb, rc)

    def ring(d, line):
        return (lax.rem(z + d + N_Z, N_Z) * 2 + line, oj, v)

    across = (z * 2 + 1 - xl, oj, v)
    sibling = (oi, yy * 2 + 1 - c, v)
    peer = (oi, oj, 1 - v)
    diag = [(oj * 2 + p) == oi for p in range(2)]

    def pair(p, w):
        return (oj * 2 + p, oi // 2, w)

    barrier = pltpu.get_barrier_semaphore()
    near = [ring(d, xl) for d in STEPS] + [across, sibling, peer]
    if any(EARLY):
        near += [ring(d, 1 - xl) for d in STEPS]
    for who in near:
        pl.semaphore_signal(barrier, inc=1, device_id=who, device_id_type=MESH)

    hub = oj == z
    for line in range(2):
        for w in range(2):
            @pl.when(jnp.logical_not(hub & (line == xl) & (w == v)))
            def _(line=line, w=w):
                pl.semaphore_signal(barrier, inc=1, device_id=(z * 2 + line, z, w), device_id_type=MESH)

    own_copy = pltpu.make_async_copy(slabs, own, own_sem)
    own_copy.start()
    small = []
    for k, (src, dst) in enumerate((
            (occ_bins_in, occ_bins), (vir_bins_in, vir_bins), (occ_levels_in, occ_levels), (vir_levels_in, vir_levels))):
        cp = pltpu.make_async_copy(src, dst, small_sem.at[k])
        cp.start()
        small.append(cp)
    own_copy.wait()
    wide_own = own[...].astype(jnp.float32)
    lane = lax.broadcasted_iota(jnp.int32, (80, LANES), 1)
    left = aux - 2 * LANES
    half_left = left // 2
    tail = jnp.zeros((80, LANES), jnp.float32)
    for a in range(virt):
        rows = wide_own[:, a, :]
        rows = jnp.concatenate([rows, jnp.zeros((80 - span, aux), jnp.float32)], axis=0)
        main = jnp.where(v == 0, rows[:, :LANES], rows[:, LANES : 2 * LANES])
        bufs[a // 2][a % 2, xl, 0] = main.astype(jnp.bfloat16)
        rest = jnp.concatenate([rows[:, 2 * LANES :], jnp.zeros((80, LANES - left), jnp.float32)], axis=1)
        first = pltpu.roll(rest, TAIL * a, 1) if a else rest
        second = pltpu.roll(rest, (TAIL * a - half_left) % LANES, 1)
        moved = jnp.where(v == 0, first, second)
        tail = jnp.where((lane >= TAIL * a) & (lane < TAIL * a + half_left), moved, tail)
    rc[0, xl, 0] = tail[:48].astype(jnp.bfloat16)
    rc[1, xl, 0] = jnp.concatenate([tail[48:], jnp.zeros((16, LANES), jnp.float32)], axis=0).astype(jnp.bfloat16)

    pl.semaphore_wait(barrier, len(near) + 31 * hub.astype(jnp.int32))

    def remote(src, dst, s, r, who):
        cp = pltpu.make_async_remote_copy(
            src_ref=src, dst_ref=dst, send_sem=s, recv_sem=r, device_id=who, device_id_type=MESH)
        cp.start()
        return cp

    sent = []

    def send(src, dst, s, r, who):
        sent.append(remote(src, dst, s, r, who))
        return sent[-1]

    x_copies = [[None] * 3 for _ in bufs]
    c_copies = [[] for _ in bufs]
    z_first, z_second = {}, {}

    def to_sibling(n, block):
        k = len(c_copies[n])
        c_copies[n].append(send(block, block, cs.at[n, k], cr.at[n, k], sibling))

    def x_send(n, g):
        lo, hi = GROUPS[g]
        block = bufs[n].at[c, xl, pl.ds(lo, hi - lo)]
        x_copies[n][g] = send(block, block, xs.at[n, g], xr.at[n, g], across)

    def start(n):
        buf, row = bufs[n], []
        for k, d in enumerate(STEPS):
            row.append(send(buf.at[c, xl, 0], buf.at[c, xl, place_of(-d % N_Z)], zs.at[n, k], zr.at[n, k], ring(d, xl)))
        x_send(n, 0)
        if EARLY[n]:
            for k, d in enumerate(STEPS):
                row.append(send(
                    buf.at[c, xl, 0], buf.at[c, xl, place_of(-d % N_Z)], zs.at[n, 7 + k], zr.at[n, 7 + k], ring(d, 1 - xl)))
        z_first[n] = row

    def after_first(n):
        buf = bufs[n]
        for cp in z_first[n][:2]:
            cp.wait_recv()
        lines = pl.ds(0, 2) if EARLY[n] else pl.ds(xl, 1)
        back, ahead = place_of(6), place_of(2)
        row = [
            send(buf.at[c, lines, back], buf.at[c, lines, place_of(5)], zs.at[n, 4], zr.at[n, 4], ring(1, xl)),
            send(buf.at[c, lines, ahead], buf.at[c, lines, place_of(3)], zs.at[n, 5], zr.at[n, 5], ring(-1, xl)),
            send(buf.at[c, lines, back + c * (ahead - back)], buf.at[c, lines, place_of(4)],
                 zs.at[n, 6], zr.at[n, 6], ring(2 - 4 * c, xl)),
        ]
        z_second[n] = row
        for cp in z_first[n][2:]:
            cp.wait_recv()
        if not EARLY[n]:
            x_send(n, 1)
        to_sibling(n, buf.at[c, lines, pl.ds(1, 4)])

    def after_second(n):
        buf = bufs[n]
        for cp in z_second[n]:
            cp.wait_recv()
        lines = pl.ds(0, 2) if EARLY[n] else pl.ds(xl, 1)
        if not EARLY[n]:
            x_send(n, 2)
        to_sibling(n, buf.at[c, lines, pl.ds(5, 3)])

    def after_x(n, g):
        x_copies[n][g].wait_recv()
        lo, hi = GROUPS[g]
        to_sibling(n, bufs[n].at[c, 1 - xl, pl.ds(lo, hi - lo)])

    def after_c(n):
        for cp in c_copies[n]:
            cp.wait_recv()
        buf = bufs[n]
        for zz in range(N_Z):
            pos = place_of(lax.rem(zz - z + N_Z, N_Z))
            for half in range(2):
                at = (2 * zz + half) * span
                if n < 2:
                    for k in range(2):
                        bf[2 * n + k, at : at + span, :] = buf[k, half, pos][:span].astype(jnp.float32)
                else:
                    bf[4, at : at + 48, :] = buf[0, half, pos].astype(jnp.float32)
                    bf[4, at + 48 : at + span, :] = buf[1, half, pos][: span - 48].astype(jnp.float32)
        for a in range(2 * n, min(2 * n + 2, 5)):
            bc[:, LANES * a : LANES * (a + 1)] = bf[a].astype(jnp.bfloat16)

    def fold(x):
        return jnp.sum(x.reshape(full // 8, 8, LANES), axis=0)

    def product(p, n):
        cols = slice(256 * n, min(256 * n + 256, 5 * LANES))
        return jnp.dot(t[p], bc[:, cols], preferred_element_type=jnp.float32)

    def contract_tail():
        for p in range(2):
            part = product(p, 2)
            for d in range(4):
                acc[p, 4, d] = fold(part * (pltpu.roll(bf[4], TAIL * d, 1) if d else bf[4]))

    for n in (0, 1, 2):
        start(n)
    t_copies = []
    for p in range(2):
        cp = pltpu.make_async_copy(amps.at[0, p], t.at[p], t_sem.at[p])
        cp.start()
        t_copies.append(cp)
    after_first(0)
    after_first(1)
    after_first(2)
    after_second(0)
    after_second(1)
    after_second(2)
    after_x(0, 0)
    after_x(1, 0)
    after_x(2, 0)
    after_x(0, 1)
    after_x(1, 1)
    after_x(2, 1)
    after_x(0, 2)
    after_x(1, 2)
    after_x(2, 2)
    for cp in t_copies:
        cp.wait()
    after_c(0)
    after_c(1)
    after_c(2)
    for n in range(2):
        for p in range(2):
            part = product(p, n)
            for k in range(2):
                for a in range(4):
                    acc[p, a, 2 * n + k] = fold(part[:, LANES * k : LANES * (k + 1)] * bf[a])
    contract_tail()

    lane = lax.broadcasted_iota(jnp.int32, (8, LANES), 1)
    wide = lax.broadcasted_iota(jnp.int32, (16, LANES), 1)
    row = lax.broadcasted_iota(jnp.int32, (16, LANES), 0)
    keep = (wide == row) | (wide == 16 + 4 * (row % 4) + row // 4)
    for p in range(2):
        rows = []
        for a in range(4):
            for b in range(4):
                inside = (lane >= TAIL * b) & (lane < TAIL * (b + 1))
                total = acc[p, a, b] + jnp.where(inside, acc[p, 4, (b - a) % 4], 0.0)
                rows.append(jnp.sum(total, axis=0, keepdims=True))
        total = jnp.sum(jnp.concatenate(rows, axis=0), axis=1, keepdims=True)
        mine[p] = jnp.broadcast_to(jnp.sum(jnp.where(keep, total, 0.0), axis=0, keepdims=True), (8, LANES))

    place = oi % 2
    for p in range(2):
        remote(mine.at[p], from_pair.at[place, v], fs.at[2 * p + 1], fr.at[place, v], pair(p, 1 - v))

        @pl.when(jnp.logical_not(diag[p]))
        def _(p=p):
            remote(mine.at[p], from_pair.at[place, v], fs.at[2 * p], fr.at[place, v], pair(p, v))

        @pl.when(diag[p])
        def _(p=p):
            pltpu.make_async_copy(mine.at[p], from_pair.at[p, v], fr.at[p, v]).start()

    to_vert = remote(mine, from_vert, fs.at[4], fr.at[2, 0], peer)
    sent.append(to_vert)

    for cp in small:
        cp.wait()
    energy_i = occ_levels[occ_bins[oi]]
    ea = jnp.zeros((8, LANES), jnp.float32)
    eb = jnp.zeros((8, LANES), jnp.float32)
    for k in range(4):
        level = vir_levels[vir_bins[k]]
        ea = jnp.where(lane // 4 == k, level, ea)
        eb = jnp.where(lane % 4 == k, level, eb)

    to_vert.wait_recv()
    for p in range(2):
        for w in range(2):
            pltpu.make_async_copy(from_pair.at[p, w], from_pair.at[p, w], fr.at[p, w]).wait()
        here = mine[p] + from_vert[p]
        there = from_pair[p, 0] + from_pair[p, 1]
        denom = energy_i + occ_levels[occ_bins[oj * 2 + p]] - ea - eb
        new = (here + pltpu.roll(there, LANES - 16, 1)) / denom
        swapped = (there + pltpu.roll(here, LANES - 16, 1)) / denom
        two = 2.0 * new - swapped

        def spread(x):
            x = jnp.where(v == 0, x, pltpu.roll(x, LANES - 8, 1))
            x = jnp.where(lax.broadcasted_iota(jnp.int32, (8, LANES), 0) == 0, x, pltpu.roll(x, LANES - 4, 1))
            return x[:2, :4]

        out[0, 0, p] = spread(new)
        out[1, 0, p] = spread(swapped)

    for cp in sent:
        cp.wait_send()
    for p in range(2):
        pltpu.make_async_copy(mine.at[p], mine.at[p], fs.at[2 * p + 1]).wait()

        @pl.when(jnp.logical_not(diag[p]))
        def _(p=p):
            pltpu.make_async_copy(mine.at[p], mine.at[p], fs.at[2 * p]).wait()


def on_device(amplitudes, slabs, occ_bins, vir_bins, occ_levels, vir_levels):
    full = amplitudes.shape[2]
    bf16, f32 = jnp.bfloat16, jnp.float32
    dma, vmem = pltpu.SemaphoreType.DMA, pltpu.VMEM
    any_space = pl.BlockSpec(memory_space=pltpu.HBM)
    smem = pltpu.SMEM
    both = pl.pallas_call(
        kernel,
        out_shape=pltpu.VMEM((2, 1, 2, 2, 4), f32),
        in_specs=[any_space] * 6,
        out_specs=pl.BlockSpec(memory_space=pltpu.VMEM),
        scratch_shapes=[
            smem(occ_bins.shape, jnp.int32), smem(vir_bins.shape, jnp.int32),
            smem(occ_levels.shape, f32), smem(vir_levels.shape, f32),
            dma((4,)),
            vmem((2, full, full), bf16),
            vmem((slabs.shape[1], slabs.shape[0], slabs.shape[2]), bf16),
            vmem((2, 2, N_Z, 80, LANES), bf16),
            vmem((2, 2, N_Z, 80, LANES), bf16),
            vmem((2, 2, N_Z, 48, LANES), bf16),
            vmem((5, full, LANES), f32),
            vmem((full, 5 * LANES), bf16),
            vmem((2, 5, 4, 8, LANES), f32),
            vmem((2, 8, LANES), f32),
            vmem((2, 8, LANES), f32),
            vmem((2, 2, 8, LANES), f32),
            dma((2,)), dma,
            dma((3, 11)), dma((3, 11)),
            dma((3, 3)), dma((3, 3)),
            dma((3, 5)), dma((3, 5)),
            dma((5,)), dma((3, 2)),
        ],
        compiler_params=pltpu.CompilerParams(
            collective_id=0, has_side_effects=True, vmem_limit_bytes=56 << 20),
    )(amplitudes, jnp.transpose(slabs, (1, 0, 2)), occ_bins, vir_bins, occ_levels, vir_levels)
    return both[0], (2.0 * both[0] - both[1]).astype(bf16)


def solution(mesh):
    return jax.shard_map(
        on_device,
        mesh=mesh,
        in_specs=(P("oi", "oj", None, None), P(None, "oi", None), P(), P(), P(), P()),
        out_specs=(P("oi", "oj", "vert", None), P("oi", "oj", "vert", None)),
        check_vma=False,
    )
```
